512 devices in a mesh: gene: 32 (over z_hi, y), cell: 16 (over z_lo, x, core).
Axes of the slice: x: 4, y: 8, z: 8 (z_hi: 4, z_lo: 2; z = z_hi * 2 + z_lo), core: 2. Of those that a mesh axis runs over, the one named last changes fastest.
Arguments:
- expression: float32 [4096, 12288], P('cell', 'gene'), may hold values from -40 to 48
Outputs:
- band: float32 [12288, 2688], P(('gene', 'cell'))
The draws below stay inside these ranges and needn't reach their ends.
All inputs are finite; a program needn't handle non-finite values.
Results may differ from the reference program's by a relative error of at most 0.00065.
Values may be sent and summed in bfloat16 or wider, within the bound.
A program may use at most 64 MiB of HBM per device.

```python
import jax
import jax.numpy as jnp
from jax import lax

GENE_DEV = 384
SLICES = 4
REACH = 3
GENES = 12288
CELLS = 4096
BAND = 2688
N_GENE = 32


def draw_expression(key, part):
    key = jax.random.fold_in(key, 7)
    noise_key, level_key = jax.random.split(key)
    noise = jnp.clip(jax.random.normal(noise_key, (CELLS, GENES), jnp.float32), -5.0, 5.0)
    mixed = noise + 0.7 * jnp.roll(noise, GENE_DEV, axis=1)
    mixed = mixed + 0.5 * jnp.roll(noise, -2 * GENE_DEV - 1, axis=1)
    mixed = mixed + 0.4 * jnp.roll(noise, 3 * GENE_DEV + 2, axis=1)
    level = jax.random.uniform(level_key, (GENES,), jnp.float32, 0.5, 3.0)
    depth = 1.0 + 2.0 * jnp.arange(CELLS, dtype=jnp.float32) / (CELLS - 1)
    return (depth[:, None] * (level[None, :] + mixed)).astype(jnp.float32)


def setup_inputs(seed: int = 0) -> dict:
    arg_keys = jax.random.split(jax.random.key(seed), 2)
    expression = draw_expression(jax.random.fold_in(arg_keys[1], 71), 0)
    return {"expression": expression}


EPS = 1e-05
RADIX = 4.0

def slice_panels(standard, scale):
    rest = standard * scale
    pieces = []
    for level in range(SLICES):
        grown = rest * RADIX
        piece = jnp.floor(grown)
        pieces.append(piece)
        rest = grown - piece
    return jnp.stack(pieces)

def reference(expression):
    count = expression.shape[0]
    mean = lax.optimization_barrier(jnp.sum(expression, axis=0)) / count
    centred = expression - mean
    spread = lax.optimization_barrier(jnp.sum(centred * centred, axis=0))
    standard = centred / jnp.sqrt(spread / count + EPS)
    peak = lax.optimization_barrier(jnp.max(jnp.abs(standard), axis=0))
    scale = jnp.exp2(-jnp.ceil(jnp.log2(peak)))
    panels = slice_panels(standard, scale)
    partner = []
    for first in range(SLICES):
        total = jnp.zeros_like(panels[0])
        for second in range(SLICES - first):
            total = total + panels[second] * RADIX ** (-(second + 1))
        partner.append(total)
    partner = jnp.stack(partner)
    reach = REACH * GENE_DEV
    extended = jnp.concatenate([partner[:, :, GENES - reach:], partner, partner[:, :, :reach]], axis=2)
    scale_ext = jnp.concatenate([scale[GENES - reach:], scale, scale[:reach]])
    weights = jnp.array([RADIX ** (-(level + 1)) for level in range(SLICES)], jnp.float32)

    def one_block(index):
        start = (index * GENE_DEV).astype(jnp.int32)
        rows = lax.dynamic_slice_in_dim(panels, start, GENE_DEV, 2) * weights[:, None, None]
        columns = lax.dynamic_slice_in_dim(extended, start, BAND, 2)
        product = jnp.einsum('scg,sch->gh', rows, columns, precision=lax.Precision.HIGHEST)
        row_scale = lax.dynamic_slice_in_dim(scale, start, GENE_DEV, 0)
        col_scale = lax.dynamic_slice_in_dim(scale_ext, start, BAND, 0)
        return product / (row_scale[:, None] * col_scale[None, :] * count)
    blocks = lax.map(one_block, jnp.arange(N_GENE, dtype=jnp.int32))
    return blocks.reshape(GENES, BAND)
```

```python
import jax
import jax.numpy as jnp
from jax import lax
from jax.experimental import pallas as pl
from jax.experimental.pallas import tpu as pltpu
from jax.sharding import PartitionSpec as P

EPS = 1e-05
MESH = pl.DeviceIdType.MESH
N_GENE, N_CELL, N_CHIP = 32, 16, 8
GENES, CELLS, ROWS = 384, 256, 24
TOTAL = float(CELLS * N_CELL)
CARRY = GENES + 16
UNITS = 7


def power_of_two(power):
    size = jnp.abs(power).astype(jnp.int32)
    up = jnp.ones_like(power)
    down = jnp.ones_like(power)
    for bit in range(7):
        on = (size & (1 << bit)) != 0
        up = jnp.where(on, up * 2.0 ** (1 << bit), up)
        down = jnp.where(on, down * 2.0 ** -(1 << bit), down)
    return jnp.where(power < 0, down, up)


def lanes(rows):
    return jnp.concatenate([rows[i : i + 1] for i in range(3)], axis=1)


def kernel(
    x_hbm, out_ref, x_ref, stat, gathered, own, partner, left, right, unscaled, prod, sibling,
    paired, arrived, turned, crossed, row_scale, x_sem, stat_sems, gene_send, gene_recv,
    core_send, core_recv, sum_send, sum_recv, turn_send, turn_recv,
):
    gene = lax.axis_index("gene")
    cell = lax.axis_index("cell")
    core = lax.rem(cell, 2)
    chip = lax.div(cell, 2)
    even = lax.rem(gene, 2) == 0
    here = [jnp.where(even, a, b) for a, b in ((1, 3), (-1, -3), (2, -2))]
    away = [jnp.where(even, a, b) for a, b in ((-3, -1), (3, 1), (-2, 2))]

    def at(offset):
        return lax.rem(gene + offset + N_GENE, N_GENE)

    barrier = pltpu.get_barrier_semaphore()
    for step in range(1, N_CELL):
        pl.semaphore_signal(
            barrier, inc=1, device_id=(gene, lax.rem(cell + step, N_CELL)), device_id_type=MESH
        )
    for offset in (1, -1, 2, -2, 3, -3):
        pl.semaphore_signal(barrier, inc=1, device_id=(at(offset), cell), device_id_type=MESH)

    load = pltpu.make_async_copy(x_hbm, x_ref, x_sem)
    load.start()
    load.wait()
    x = x_ref[...]
    mean = jnp.sum(x, axis=0, keepdims=True) * (1.0 / CELLS)
    centred = x - mean
    rows = [
        mean,
        jnp.sum(centred * centred, axis=0, keepdims=True),
        jnp.max(x, axis=0, keepdims=True),
        jnp.min(x, axis=0, keepdims=True),
    ]
    parts = [row[:, 128 * i : 128 * i + 128] for row in rows for i in range(3)]
    stat[...] = jnp.concatenate(parts + [jnp.zeros((4, 128), jnp.float32)], axis=0)
    gathered[cell] = stat[...]

    pl.semaphore_wait(barrier, 21)

    for step in range(1, N_CELL):
        pltpu.make_async_remote_copy(
            src_ref=stat,
            dst_ref=gathered.at[cell],
            send_sem=stat_sems.at[0],
            recv_sem=stat_sems.at[1],
            device_id=(gene, lax.rem(cell + step, N_CELL)),
            device_id_type=MESH,
        ).start()
    many = gathered.at[pl.ds(0, N_CELL - 1)]
    pltpu.make_async_copy(many, many, stat_sems.at[1]).wait()

    total = gathered[0][0:3]
    for i in range(1, N_CELL):
        total = total + gathered[i][0:3]
    mean3 = total * (1.0 / N_CELL)
    inner = jnp.zeros_like(mean3)
    outer = jnp.zeros_like(mean3)
    high = gathered[0][6:9]
    low = gathered[0][9:12]
    for i in range(N_CELL):
        inner = inner + gathered[i][3:6]
        shift = gathered[i][0:3] - mean3
        outer = outer + shift * shift
        high = jnp.maximum(high, gathered[i][6:9])
        low = jnp.minimum(low, gathered[i][9:12])
    spread = inner + outer * float(CELLS)
    deviation = jnp.sqrt(spread * (1.0 / TOTAL) + EPS)
    peak = jnp.maximum(jnp.abs((high - mean3) / deviation), jnp.abs((low - mean3) / deviation))
    power3 = jnp.ceil(jnp.log2(peak))
    scale3 = power_of_two(-power3)
    power = lanes(power3)
    gain = power_of_two(power)

    standard = (x_ref[...] - lanes(mean3)) / lanes(deviation)
    value = jnp.floor((standard * lanes(scale3)) * 256.0)
    turned_value = value.T
    unscaled[...] = turned_value
    own[0:GENES, :] = turned_value.astype(jnp.bfloat16)
    second = jnp.concatenate([power[:, 256:384], jnp.zeros((1, 128), jnp.float32)], axis=1)
    own[GENES:CARRY, :] = jnp.concatenate(
        [power[:, 0:256], second, jnp.zeros((14, 256), jnp.float32)], axis=0
    ).astype(jnp.bfloat16)

    gene_copies = []
    for slot in range(3):
        copy = pltpu.make_async_remote_copy(
            src_ref=own,
            dst_ref=partner.at[slot],
            send_sem=gene_send.at[slot],
            recv_sem=gene_recv.at[slot],
            device_id=(at(away[slot]), cell),
            device_id_type=MESH,
        )
        copy.start()
        gene_copies.append(copy)

    wide = jnp.broadcast_to(gain * (2.0**-10 / TOTAL), (128, GENES)).T
    row_scale[...] = jnp.concatenate([wide, wide, wide], axis=1)

    def panels(value, slices_ref, sums_ref):
        fourth = value
        third = jnp.floor(fourth * 0.25)
        second = jnp.floor(third * 0.25)
        first = jnp.floor(second * 0.25)
        if slices_ref is not None:
            slices_ref[:, 0:256] = first.astype(jnp.bfloat16)
            slices_ref[:, 256:512] = (second - 4.0 * first).astype(jnp.bfloat16)
            slices_ref[:, 512:768] = (third - 4.0 * second).astype(jnp.bfloat16)
            slices_ref[:, 768:1024] = (fourth - 4.0 * third).astype(jnp.bfloat16)
        sums_ref[:, 0:256] = fourth.astype(jnp.bfloat16)
        sums_ref[:, 256:512] = third.astype(jnp.bfloat16)
        sums_ref[:, 512:768] = second.astype(jnp.bfloat16)
        sums_ref[:, 768:1024] = first.astype(jnp.bfloat16)

    core_copies, sum_copies, turn_copies = {}, {}, {}

    def multiply(unit, a_ref, b_ref):
        c = lax.dot_general(
            a_ref[...], b_ref[...], (((1,), (1,)), ((), ())), preferred_element_type=jnp.float32
        )
        prod[unit] = c.reshape(N_CHIP, 2, ROWS, GENES)
        copy = pltpu.make_async_remote_copy(
            src_ref=prod.at[unit, :, 1 - core],
            dst_ref=sibling.at[unit],
            send_sem=core_send.at[unit],
            recv_sem=core_recv.at[unit],
            device_id=(gene, chip * 2 + 1 - core),
            device_id_type=MESH,
        )
        copy.start()
        core_copies[unit] = copy

    def pair_up(unit):
        core_copies[unit].wait_recv()
        paired[unit] = prod[unit, :, core] + sibling[unit]
        for step in range(1, N_CHIP):
            there = lax.rem(chip + step, N_CHIP)
            copy = pltpu.make_async_remote_copy(
                src_ref=paired.at[unit, there],
                dst_ref=arrived.at[unit, step - 1],
                send_sem=sum_send.at[unit],
                recv_sem=sum_recv.at[unit],
                device_id=(gene, there * 2 + core),
                device_id_type=MESH,
            )
            copy.start()

    def summed(unit):
        pltpu.make_async_copy(arrived.at[unit], arrived.at[unit], sum_recv.at[unit]).wait()
        total = paired[unit, chip]
        for step in range(N_CHIP - 1):
            total = total + arrived[unit, step]
        return total

    mine = pl.ds(pl.multiple_of(cell * ROWS, 8), ROWS)

    def place(offset, block):
        start = pl.multiple_of((offset + 3) * GENES, 128)
        out_ref[:, pl.ds(start, GENES)] = block

    def turn(slot):
        unit = 1 + 2 * slot
        turned[slot] = summed(unit) * gain
        copy = pltpu.make_async_remote_copy(
            src_ref=turned.at[slot],
            dst_ref=crossed.at[slot],
            send_sem=turn_send.at[slot],
            recv_sem=turn_recv.at[slot],
            device_id=(at(here[slot]), cell),
            device_id_type=MESH,
        )
        copy.start()
        turn_copies[slot] = copy

    def keep(slot):
        far = partner[slot, GENES:CARRY, :].astype(jnp.float32)
        far_power = jnp.concatenate([far[0:1, :], far[1:2, 0:128]], axis=1)
        place(here[slot], summed(2 + 2 * slot) * (row_scale[mine, :] * power_of_two(far_power)))

    panels(unscaled[...], left, right.at[3])
    multiply(0, left, right.at[3])
    pair_up(0)
    for slot in range(3):
        gene_copies[slot].wait_recv()
        panels(partner[slot, 0:GENES, :].astype(jnp.float32), None, right.at[slot])
        multiply(1 + 2 * slot, right.at[slot], left)
        multiply(2 + 2 * slot, left, right.at[slot])
        pair_up(1 + 2 * slot)
        pair_up(2 + 2 * slot)
        if slot == 0:
            place(0, summed(0) * (row_scale[mine, :] * gain))
        else:
            turn(slot - 1)
            keep(slot - 1)
    turn(2)
    keep(2)
    for slot in range(3):
        turn_copies[slot].wait_recv()
        place(away[slot], crossed[slot] * row_scale[mine, :])

    pltpu.make_async_copy(many, many, stat_sems.at[0]).wait()
    for slot in range(3):
        gene_copies[slot].wait_send()
        turn_copies[slot].wait_send()
    for unit in range(UNITS):
        core_copies[unit].wait_send()
        pltpu.make_async_copy(arrived.at[unit], arrived.at[unit], sum_send.at[unit]).wait()


def on_device(expression):
    f32, bf16 = jnp.float32, jnp.bfloat16
    vmem, dma = pltpu.VMEM, pltpu.SemaphoreType.DMA
    return pl.pallas_call(
        kernel,
        out_shape=jax.ShapeDtypeStruct((ROWS, UNITS * GENES), f32),
        in_specs=[pl.BlockSpec(memory_space=pl.ANY)],
        out_specs=pl.BlockSpec(memory_space=pltpu.VMEM),
        scratch_shapes=[
            vmem((CELLS, GENES), f32),
            vmem((16, 128), f32),
            vmem((N_CELL, 16, 128), f32),
            vmem((CARRY, CELLS), bf16),
            vmem((3, CARRY, CELLS), bf16),
            vmem((GENES, 4 * CELLS), bf16),
            vmem((4, GENES, 4 * CELLS), bf16),
            vmem((GENES, CELLS), f32),
            vmem((UNITS, N_CHIP, 2, ROWS, GENES), f32),
            vmem((UNITS, N_CHIP, ROWS, GENES), f32),
            vmem((UNITS, N_CHIP, ROWS, GENES), f32),
            vmem((UNITS, N_CHIP - 1, ROWS, GENES), f32),
            vmem((3, ROWS, GENES), f32),
            vmem((3, ROWS, GENES), f32),
            vmem((GENES, GENES), f32),
            dma,
            dma((2,)),
            dma((3,)),
            dma((3,)),
            dma((UNITS,)),
            dma((UNITS,)),
            dma((UNITS,)),
            dma((UNITS,)),
            dma((3,)),
            dma((3,)),
        ],
        compiler_params=pltpu.CompilerParams(
            collective_id=0, has_side_effects=True, vmem_limit_bytes=48 * 1024 * 1024
        ),
        name="banded_correlation",
    )(expression)


def solution(mesh):
    return jax.shard_map(
        on_device,
        mesh=mesh,
        in_specs=(P("cell", "gene"),),
        out_specs=P(("gene", "cell"), None),
        check_vma=False,
    )
```

```python
import jax
import jax.numpy as jnp
from jax import lax
from jax.experimental import pallas as pl
from jax.experimental.pallas import tpu as pltpu
from jax.sharding import PartitionSpec as P

EPS = 1e-05
MESH = pl.DeviceIdType.MESH
N_GENE, N_CELL, N_CHIP, N_X = 32, 16, 8, 4
GENES, CELLS, ROWS, PART = 384, 256, 24, 96
TOTAL = float(CELLS * N_CELL)
SLOTS = 3
NEAR = (1, -1, 2, -2, 3, -3)


def power_of_two(power):
    size = jnp.abs(power).astype(jnp.int32)
    up = jnp.ones_like(power)
    down = jnp.ones_like(power)
    for bit in range(7):
        on = (size & (1 << bit)) != 0
        up = jnp.where(on, up * 2.0 ** (1 << bit), up)
        down = jnp.where(on, down * 2.0 ** -(1 << bit), down)
    return jnp.where(power < 0, down, up)


def lanes(rows):
    return jnp.concatenate([rows[i : i + 1] for i in range(3)], axis=1)


def kernel(
    x_hbm, out_ref, x_ref, gathered, block, sent, flat, powers, far_powers, partner, left, right,
    prod, sibling, paired, arrived, turned, turned_sibling, turned_pair, crossed, row_scale,
    x_sem, stat_sems, block_sems, gene_send, gene_recv, power_send, power_recv,
    core_send, core_recv, sum_send, sum_recv, flip_send, flip_recv, turn_send, turn_recv,
):
    gene = lax.axis_index("gene")
    cell = lax.axis_index("cell")
    core = lax.rem(cell, 2)
    chip = lax.div(cell, 2)
    x_at = lax.rem(chip, N_X)
    z_at = lax.div(chip, N_X)
    even = lax.rem(gene, 2) == 0
    here = [jnp.where(even, a, b) for a, b in ((1, 3), (-1, -3), (2, -2))]
    away = [jnp.where(even, a, b) for a, b in ((-3, -1), (3, 1), (-2, 2))]

    def at(offset):
        return lax.rem(gene + offset + N_GENE, N_GENE)

    def rank(z, x, core):
        return z * (2 * N_X) + x * 2 + core

    def remote(src, dst, send, recv, gene_to, cell_to):
        return pltpu.make_async_remote_copy(
            src_ref=src,
            dst_ref=dst,
            send_sem=send,
            recv_sem=recv,
            device_id=(gene_to, cell_to),
            device_id_type=MESH,
        )

    def wait_bytes(ref, sem):
        pltpu.make_async_copy(ref, ref, sem).wait()

    load = pltpu.make_async_copy(x_hbm, x_ref, x_sem)
    load.start()
    barrier = pltpu.get_barrier_semaphore()

    def greet(gene_to, cell_to):
        pl.semaphore_signal(barrier, inc=1, device_id=(gene_to, cell_to), device_id_type=MESH)

    for step in range(1, N_CELL):
        greet(gene, lax.rem(cell + step, N_CELL))
    for offset in NEAR:
        for x in range(N_X):
            greet(at(offset), rank(z_at, x, core))
        greet(at(offset), rank(1 - z_at, x_at, core))

    load.wait()
    x = x_ref[...]
    mean = jnp.sum(x, axis=0, keepdims=True) * (1.0 / CELLS)
    centred = x - mean
    rows = [
        mean,
        jnp.sum(centred * centred, axis=0, keepdims=True),
        jnp.max(x, axis=0, keepdims=True),
        jnp.min(x, axis=0, keepdims=True),
    ]
    parts = [row[:, 128 * i : 128 * i + 128] for row in rows for i in range(3)]
    gathered[cell] = jnp.concatenate(parts + [jnp.zeros((4, 128), jnp.float32)], axis=0)

    pl.semaphore_wait(barrier, N_CELL - 1 + len(NEAR) * (N_X + 1))

    for step in range(1, N_CELL):
        remote(
            gathered.at[cell], gathered.at[cell], stat_sems.at[0], stat_sems.at[1],
            gene, lax.rem(cell + step, N_CELL),
        ).start()
    many = gathered.at[pl.ds(0, N_CELL - 1)]
    wait_bytes(many, stat_sems.at[1])

    total = gathered[0][0:3]
    for i in range(1, N_CELL):
        total = total + gathered[i][0:3]
    mean3 = total * (1.0 / N_CELL)
    inner = jnp.zeros_like(mean3)
    outer = jnp.zeros_like(mean3)
    high = gathered[0][6:9]
    low = gathered[0][9:12]
    for i in range(N_CELL):
        inner = inner + gathered[i][3:6]
        shift = gathered[i][0:3] - mean3
        outer = outer + shift * shift
        high = jnp.maximum(high, gathered[i][6:9])
        low = jnp.minimum(low, gathered[i][9:12])
    spread = inner + outer * float(CELLS)
    deviation = jnp.sqrt(spread * (1.0 / TOTAL) + EPS)
    peak = jnp.maximum(jnp.abs((high - mean3) / deviation), jnp.abs((low - mean3) / deviation))
    power3 = jnp.ceil(jnp.log2(peak))
    scale3 = power_of_two(-power3)
    gain3 = power_of_two(power3)
    gain = lanes(gain3)

    standard = (x_ref[...] - lanes(mean3)) / lanes(deviation)
    value = jnp.floor((standard * lanes(scale3)) * 256.0)
    block[x_at] = value.astype(jnp.bfloat16)
    sent[...] = value.T.astype(jnp.bfloat16).reshape(2, GENES // 2, CELLS)
    powers[...] = jnp.concatenate([gain3, jnp.zeros((5, 128), jnp.float32)], axis=0)

    mine = block.at[x_at]
    for step in (1, 3, 2):
        there = lax.rem(x_at + step, N_X)
        remote(
            mine, mine, block_sems.at[0], block_sems.at[1], gene, rank(z_at, there, core)
        ).start()
    for slot in range(SLOTS):
        for step in range(N_X):
            there = lax.rem(x_at + step, N_X)
            start = pl.multiple_of(there * (PART // 2), 16)
            remote(
                sent.at[:, pl.ds(start, PART // 2)], partner.at[slot, x_at],
                gene_send.at[slot], gene_recv.at[slot], at(away[slot]), rank(z_at, there, core),
            ).start()
        remote(
            powers, far_powers.at[slot], power_send.at[slot], power_recv.at[slot],
            at(away[slot]), cell,
        ).start()

    wide = jnp.broadcast_to(gain * (2.0**-10 / TOTAL), (128, GENES)).T
    row_scale[...] = jnp.concatenate([wide, wide, wide], axis=1)
    mine_rows = pl.ds(pl.multiple_of(cell * ROWS, 8), ROWS)

    def levels(value):
        fourth = value.astype(jnp.float32)
        third = jnp.floor(fourth * 0.25)
        second = jnp.floor(third * 0.25)
        return fourth, third, second, jnp.floor(second * 0.25)

    wait_bytes(block.at[pl.ds(0, N_X - 1)], block_sems.at[1])
    for x in range(N_X):
        fourth, third, second, first = levels(block[x])
        slices = (first, second - 4.0 * first, third - 4.0 * second, fourth - 4.0 * third)
        for i, piece in enumerate(slices):
            start = CELLS * (4 * x + i)
            left[start : start + CELLS, :] = piece.astype(jnp.bfloat16)
        flat[x] = fourth.T.reshape(2, GENES // 2, CELLS)

    core_copies, flip_copies, turn_copies = {}, {}, {}

    def multiply(unit, pieces):
        for x in range(N_X):
            for i, piece in enumerate(levels(pieces(x))):
                start = CELLS * (4 * x + i)
                right[unit, :, start : start + CELLS] = piece.astype(jnp.bfloat16)
        c = jnp.dot(right[unit], left[...], preferred_element_type=jnp.float32)
        if unit < SLOTS:
            turned[unit] = (c * gain).reshape(2, 2, ROWS, GENES)
            copy = remote(
                turned.at[unit, :, 1 - core], turned_sibling.at[unit],
                flip_send.at[unit], flip_recv.at[unit], gene, rank(z_at, x_at, 1 - core),
            )
            copy.start()
            flip_copies[unit] = copy
        prod[unit] = c.T.reshape(N_CHIP, 2, ROWS, PART)
        copy = remote(
            prod.at[unit, :, 1 - core], sibling.at[unit],
            core_send.at[unit], core_recv.at[unit], gene, rank(z_at, x_at, 1 - core),
        )
        copy.start()
        core_copies[unit] = copy

    def pair_up(unit):
        if unit < SLOTS:
            flip_copies[unit].wait_recv()
            turned_pair[unit] = turned[unit, :, core] + turned_sibling[unit]
            turn_copies[unit] = []
            for z in range(2):
                copy = remote(
                    turned_pair.at[unit, z], crossed.at[unit, z_at],
                    turn_send.at[unit], turn_recv.at[unit], at(here[unit]), rank(z, x_at, core),
                )
                copy.start()
        core_copies[unit].wait_recv()
        paired[unit] = prod[unit, :, core] + sibling[unit]
        arrived[unit, chip] = paired[unit, chip]
        for step in range(1, N_CHIP):
            there = lax.rem(chip + step, N_CHIP)
            remote(
                paired.at[unit, there], arrived.at[unit, chip],
                sum_send.at[unit], sum_recv.at[unit], gene, there * 2 + core,
            ).start()

    def place(offset, value):
        start = pl.multiple_of((offset + 3) * GENES, 128)
        out_ref[:, pl.ds(start, GENES)] = value

    def keep(unit, offset, far_gain):
        wait_bytes(arrived.at[unit, pl.ds(0, N_CHIP - 1)], sum_recv.at[unit])
        quarters = [arrived[unit, x] + arrived[unit, N_X + x] for x in range(N_X)]
        half = PART // 2
        total = jnp.concatenate(
            [q[:, half * z : half * (z + 1)] for z in range(2) for q in quarters], axis=1
        )
        place(offset, total * (row_scale[mine_rows, :] * far_gain))

    own_rows = pl.ds(pl.multiple_of(x_at * (PART // 2), 8), PART // 2)
    multiply(SLOTS, lambda x: flat[x, :, own_rows].reshape(PART, CELLS))
    pair_up(SLOTS)
    for slot in range(SLOTS):
        wait_bytes(partner.at[slot], gene_recv.at[slot])
        multiply(slot, lambda x: partner[slot, x].reshape(PART, CELLS))
        if slot:
            pair_up(slot - 1)
    pair_up(SLOTS - 1)
    keep(SLOTS, 0, gain)
    for slot in range(SLOTS):
        wait_bytes(far_powers.at[slot], power_recv.at[slot])
        keep(slot, here[slot], lanes(far_powers[slot][0:3]))
    for slot in range(SLOTS):
        wait_bytes(crossed.at[slot], turn_recv.at[slot])
        place(away[slot], (crossed[slot, 0] + crossed[slot, 1]) * row_scale[mine_rows, :])

    wait_bytes(many, stat_sems.at[0])
    wait_bytes(block.at[pl.ds(0, N_X - 1)], block_sems.at[0])
    for unit in range(SLOTS + 1):
        if unit < SLOTS:
            wait_bytes(sent, gene_send.at[unit])
            wait_bytes(powers, power_send.at[unit])
            flip_copies[unit].wait_send()
            wait_bytes(turned_pair.at[unit], turn_send.at[unit])
        core_copies[unit].wait_send()
        wait_bytes(arrived.at[unit, pl.ds(0, N_CHIP - 1)], sum_send.at[unit])


def on_device(expression):
    f32, bf16 = jnp.float32, jnp.bfloat16
    vmem, dma = pltpu.VMEM, pltpu.SemaphoreType.DMA
    units = SLOTS + 1
    return pl.pallas_call(
        kernel,
        out_shape=jax.ShapeDtypeStruct((ROWS, 7 * GENES), f32),
        in_specs=[pl.BlockSpec(memory_space=pl.ANY)],
        out_specs=pl.BlockSpec(memory_space=pltpu.VMEM),
        scratch_shapes=[
            vmem((CELLS, GENES), f32),
            vmem((N_CELL, 16, 128), f32),
            vmem((N_X, CELLS, GENES), bf16),
            vmem((2, GENES // 2, CELLS), bf16),
            vmem((N_X, 2, GENES // 2, CELLS), f32),
            vmem((8, 128), f32),
            vmem((SLOTS, 8, 128), f32),
            vmem((SLOTS, N_X, 2, PART // 2, CELLS), bf16),
            vmem((4 * CELLS * N_X, GENES), bf16),
            vmem((units, PART, 4 * CELLS * N_X), bf16),
            vmem((units, N_CHIP, 2, ROWS, PART), f32),
            vmem((units, N_CHIP, ROWS, PART), f32),
            vmem((units, N_CHIP, ROWS, PART), f32),
            vmem((units, N_CHIP, ROWS, PART), f32),
            vmem((SLOTS, 2, 2, ROWS, GENES), f32),
            vmem((SLOTS, 2, ROWS, GENES), f32),
            vmem((SLOTS, 2, ROWS, GENES), f32),
            vmem((SLOTS, 2, ROWS, GENES), f32),
            vmem((GENES, GENES), f32),
            dma,
            dma((2,)),
            dma((2,)),
            dma((SLOTS,)),
            dma((SLOTS,)),
            dma((SLOTS,)),
            dma((SLOTS,)),
            dma((units,)),
            dma((units,)),
            dma((units,)),
            dma((units,)),
            dma((SLOTS,)),
            dma((SLOTS,)),
            dma((SLOTS,)),
            dma((SLOTS,)),
        ],
        compiler_params=pltpu.CompilerParams(
            collective_id=0, has_side_effects=True, vmem_limit_bytes=60 * 1024 * 1024
        ),
        name="banded_correlation",
    )(expression)


def solution(mesh):
    return jax.shard_map(
        on_device,
        mesh=mesh,
        in_specs=(P("cell", "gene"),),
        out_specs=P(("gene", "cell"), None),
        check_vma=False,
    )
```

```python
import jax
import jax.numpy as jnp
from jax import lax
from jax.experimental import pallas as pl
from jax.experimental.pallas import tpu as pltpu
from jax.sharding import PartitionSpec as P

EPS = 1e-05
MESH = pl.DeviceIdType.MESH
N_GENE, N_CELL, N_CHIP, N_X, N_Y = 32, 16, 8, 4, 8
GENES, CELLS, ROWS, PART = 384, 256, 24, 96
TOTAL = float(CELLS * N_CELL)
SLOTS = 3
SLOT_ORDER = (0, 1, 2)
NEAR = (1, -1, 2, -2, 3, -3)


def power_of_two(power):
    size = jnp.abs(power).astype(jnp.int32)
    up = jnp.ones_like(power)
    down = jnp.ones_like(power)
    for bit in range(7):
        on = (size & (1 << bit)) != 0
        up = jnp.where(on, up * 2.0 ** (1 << bit), up)
        down = jnp.where(on, down * 2.0 ** -(1 << bit), down)
    return jnp.where(power < 0, down, up)


def lanes(rows):
    return jnp.concatenate([rows[i : i + 1] for i in range(3)], axis=1)


def kernel(
    x_hbm, out_ref, x_ref, gathered, block, flat, quarter, powers, far_powers, partner, left,
    right, turned, turned_sibling, turned_pair, crossed, prod, sibling, paired, arrived,
    begun, row_scale,
    x_sem, stat_sems, own_send, own_recv, gene_send, gene_recv, power_send, power_recv,
    core_send, core_recv, sum_send, sum_recv, flip_send, flip_recv, turn_send, turn_recv,
):
    gene = lax.axis_index("gene")
    cell = lax.axis_index("cell")
    core = lax.rem(cell, 2)
    chip = lax.div(cell, 2)
    x_at = lax.rem(chip, N_X)
    z_at = lax.div(chip, N_X)
    even = lax.rem(gene, 2) == 0
    place_y = lax.rem(gene, N_Y)

    def by_place(for_even, for_odd, **special):
        value = jnp.where(even, for_even, for_odd)
        for name, other in special.items():
            value = jnp.where(place_y == int(name[1:]), other, value)
        return value

    here = [by_place(1, 3, y7=2), by_place(-1, -3, y2=-3), by_place(2, -2, y1=1)]
    back = [by_place(0, 0, y7=1), by_place(1, 1, y2=2), by_place(2, 2, y1=0)]
    away = [by_place(-3, -1, y2=-1), by_place(3, 1, y1=-2), by_place(-2, 2, y7=3)]
    slot_there = [by_place(0, 0, y2=2), by_place(1, 1, y1=0), by_place(2, 2, y7=1)]

    def at(offset):
        return lax.rem(gene + offset + N_GENE, N_GENE)

    def rank(z, x, core):
        return z * (2 * N_X) + x * 2 + core

    def remote(src, dst, send, recv, gene_to, cell_to):
        return pltpu.make_async_remote_copy(
            src_ref=src,
            dst_ref=dst,
            send_sem=send,
            recv_sem=recv,
            device_id=(gene_to, cell_to),
            device_id_type=MESH,
        )

    def wait_bytes(ref, sem):
        pltpu.make_async_copy(ref, ref, sem).wait()

    load = pltpu.make_async_copy(x_hbm, x_ref, x_sem)
    load.start()
    barrier = pltpu.get_barrier_semaphore()

    def greet(gene_to, cell_to):
        pl.semaphore_signal(barrier, inc=1, device_id=(gene_to, cell_to), device_id_type=MESH)

    for step in range(1, N_CELL):
        greet(gene, lax.rem(cell + step, N_CELL))
    for offset in NEAR:
        for z in range(2):
            greet(at(offset), rank(z, x_at, core))

    load.wait()
    x = x_ref[...]
    mean = jnp.sum(x, axis=0, keepdims=True) * (1.0 / CELLS)
    centred = x - mean
    rows = [
        mean,
        jnp.sum(centred * centred, axis=0, keepdims=True),
        jnp.max(x, axis=0, keepdims=True),
        jnp.min(x, axis=0, keepdims=True),
    ]
    parts = [row[:, 128 * i : 128 * i + 128] for row in rows for i in range(3)]
    gathered[cell] = jnp.concatenate(parts + [jnp.zeros((4, 128), jnp.float32)], axis=0)

    pl.semaphore_wait(barrier, N_CELL - 1 + len(NEAR) * 2)

    for step in range(1, N_CELL):
        remote(
            gathered.at[cell], gathered.at[cell], stat_sems.at[0], stat_sems.at[1],
            gene, lax.rem(cell + step, N_CELL),
        ).start()
    many = gathered.at[pl.ds(0, N_CELL - 1)]
    wait_bytes(many, stat_sems.at[1])

    total = gathered[0][0:3]
    for i in range(1, N_CELL):
        total = total + gathered[i][0:3]
    mean3 = total * (1.0 / N_CELL)
    inner = jnp.zeros_like(mean3)
    outer = jnp.zeros_like(mean3)
    high = gathered[0][6:9]
    low = gathered[0][9:12]
    for i in range(N_CELL):
        inner = inner + gathered[i][3:6]
        shift = gathered[i][0:3] - mean3
        outer = outer + shift * shift
        high = jnp.maximum(high, gathered[i][6:9])
        low = jnp.minimum(low, gathered[i][9:12])
    spread = inner + outer * float(CELLS)
    deviation = jnp.sqrt(spread * (1.0 / TOTAL) + EPS)
    peak = jnp.maximum(jnp.abs((high - mean3) / deviation), jnp.abs((low - mean3) / deviation))
    power3 = jnp.ceil(jnp.log2(peak))
    scale3 = power_of_two(-power3)
    gain3 = power_of_two(power3)
    gain = lanes(gain3)

    standard = (x_ref[...] - lanes(mean3)) / lanes(deviation)
    value = jnp.floor((standard * lanes(scale3)) * 256.0)
    block[x_at] = value.astype(jnp.bfloat16)
    powers[...] = jnp.concatenate([gain3, jnp.zeros((5, 128), jnp.float32)], axis=0)

    x_of = [lax.rem(x_at + step, N_X) for step in range(N_X)]
    mine = block.at[x_at]
    for step, side in ((1, 0), (3, 1)):
        remote(
            mine, mine, own_send.at[0], own_recv.at[side], gene, rank(z_at, x_of[step], core)
        ).start()
    part_rows = pl.ds(pl.multiple_of(x_at * (PART // 2), 8), PART // 2)

    def send_quarter(step, values):
        flat[...] = values.T.reshape(2, GENES // 2, CELLS)
        quarter[step] = flat[:, part_rows].astype(jnp.bfloat16)
        for slot in range(SLOTS):
            remote(
                quarter.at[step], partner.at[slot_there[slot], step], gene_send.at[slot],
                gene_recv.at[slot_there[slot], step], at(away[slot]), cell,
            ).start()

    send_quarter(0, value)
    for slot in range(SLOTS):
        remote(
            powers, far_powers.at[slot_there[slot]], power_send.at[slot],
            power_recv.at[slot_there[slot]], at(away[slot]), cell,
        ).start()

    wide = jnp.broadcast_to(gain * (2.0**-10 / TOTAL), (128, GENES)).T
    row_scale[...] = jnp.concatenate([wide, wide, wide], axis=1)
    mine_rows = pl.ds(pl.multiple_of(cell * ROWS, 8), ROWS)

    def levels(value):
        fourth = value.astype(jnp.float32)
        third = jnp.floor(fourth * 0.25)
        second = jnp.floor(third * 0.25)
        return fourth, third, second, jnp.floor(second * 0.25)

    chunk = 4 * CELLS
    order = (0, 3, 1, 2)

    def spread_out(step, values):
        fourth, third, second, first = levels(values)
        slices = (first, second - 4.0 * first, third - 4.0 * second, fourth - 4.0 * third)
        for i, piece in enumerate(slices):
            start = chunk * order.index(step) + CELLS * i
            left[start : start + CELLS, :] = piece.astype(jnp.bfloat16)

    def sums_of(ref, row, piece, step):
        for i, level in enumerate(levels(piece.reshape(PART, CELLS))):
            start = chunk * order.index(step) + CELLS * i
            ref[row : row + PART, start : start + CELLS] = level.astype(jnp.bfloat16)

    spread_out(0, value)
    half = CELLS // 2
    for side, came, to in ((0, 3, 1), (1, 1, 3)):
        wait_bytes(block.at[0], own_recv.at[side])
        piece = block.at[x_of[came], pl.ds(side * half, half)]
        remote(
            piece, piece, own_send.at[1], own_recv.at[2 + side], gene, rank(z_at, x_of[to], core)
        ).start()
        send_quarter(came, block[x_of[came]].astype(jnp.float32))
    for step in (3, 1):
        spread_out(step, block[x_of[step]])
    for side in range(2):
        wait_bytes(block.at[0, pl.ds(0, half)], own_recv.at[2 + side])
    send_quarter(2, block[x_of[2]].astype(jnp.float32))
    spread_out(2, block[x_of[2]])

    twin = rank(z_at, x_at, 1 - core)

    copies = {}

    early = chunk * (N_X - 1)

    def product(rows, columns):
        return jnp.dot(right[rows, columns], left[columns], preferred_element_type=jnp.float32)

    def multiply(unit):
        rows = slice(PART * unit, PART * (unit + 1))
        if unit == SLOTS:
            c = product(rows, slice(None))
        else:
            c = begun[rows] + product(rows, slice(early, None))
        if unit < SLOTS:
            turned[unit] = (c * gain).reshape(2, 2, ROWS, GENES)
            copies["flip", unit] = remote(
                turned.at[unit, :, 1 - core], turned_sibling.at[unit],
                flip_send.at[unit], flip_recv.at[unit], gene, twin,
            )
            copies["flip", unit].start()
        prod[unit] = c.T.reshape(N_CHIP, 2, ROWS, PART)
        copies["core", unit] = remote(
            prod.at[unit, :, 1 - core], sibling.at[unit],
            core_send.at[unit], core_recv.at[unit], gene, twin,
        )
        copies["core", unit].start()

    def pair_up(unit):
        if unit < SLOTS:
            copies["flip", unit].wait_recv()
            turned_pair[unit] = turned[unit, :, core] + turned_sibling[unit]
            for z in range(2):
                remote(
                    turned_pair.at[unit, z], crossed.at[back[unit], z_at], turn_send.at[unit],
                    turn_recv.at[back[unit]], at(here[unit]), rank(z, x_at, core),
                ).start()
        copies["core", unit].wait_recv()
        paired[unit] = prod[unit, :, core] + sibling[unit]
        arrived[unit, chip] = paired[unit, chip]
        for step in range(1, N_CHIP):
            there = lax.rem(chip + step, N_CHIP)
            remote(
                paired.at[unit, there], arrived.at[unit, chip],
                sum_send.at[unit], sum_recv.at[unit], gene, there * 2 + core,
            ).start()

    for step in order:
        sums_of(right, PART * SLOTS, quarter[step], step)
    multiply(SLOTS)

    def take(slot, step):
        wait_bytes(partner.at[slot, step], gene_recv.at[slot, step])
        sums_of(right, PART * slot, partner[slot, step], step)

    for step in order[:-1]:
        for slot in SLOT_ORDER:
            take(slot, step)
    begun[...] = product(slice(0, PART * SLOTS), slice(0, early))
    for i, slot in enumerate(SLOT_ORDER):
        take(slot, order[-1])
        multiply(slot)
        pair_up(SLOT_ORDER[i - 1] if i else SLOTS)
    pair_up(SLOT_ORDER[-1])

    def place(offset, value):
        start = pl.multiple_of((offset + 3) * GENES, 128)
        out_ref[:, pl.ds(start, GENES)] = value

    others = pl.ds(0, N_CHIP - 1)

    def keep(unit, offset, far_gain):
        wait_bytes(arrived.at[unit, others], sum_recv.at[unit])
        quarters = [arrived[unit, x] + arrived[unit, N_X + x] for x in range(N_X)]
        size = PART // 2
        total = jnp.concatenate(
            [q[:, size * z : size * (z + 1)] for z in range(2) for q in quarters], axis=1
        )
        place(offset, total * (row_scale[mine_rows, :] * far_gain))

    keep(SLOTS, 0, gain)
    for slot in SLOT_ORDER:
        wait_bytes(far_powers.at[slot], power_recv.at[slot])
        keep(slot, here[slot], lanes(far_powers[slot][0:3]))
    for slot in range(SLOTS):
        wait_bytes(crossed.at[slot], turn_recv.at[slot])
        place(away[slot], (crossed[slot, 0] + crossed[slot, 1]) * row_scale[mine_rows, :])

    wait_bytes(many, stat_sems.at[0])
    wait_bytes(block.at[pl.ds(0, 2)], own_send.at[0])
    wait_bytes(block.at[0], own_send.at[1])
    for unit in range(SLOTS + 1):
        if unit < SLOTS:
            wait_bytes(quarter, gene_send.at[unit])
            wait_bytes(powers, power_send.at[unit])
            wait_bytes(turned_pair.at[unit], turn_send.at[unit])
            copies["flip", unit].wait_send()
        copies["core", unit].wait_send()
        wait_bytes(arrived.at[unit, others], sum_send.at[unit])


def on_device(expression):
    f32, bf16 = jnp.float32, jnp.bfloat16
    vmem, dma = pltpu.VMEM, pltpu.SemaphoreType.DMA
    return pl.pallas_call(
        kernel,
        out_shape=jax.ShapeDtypeStruct((ROWS, 7 * GENES), f32),
        in_specs=[pl.BlockSpec(memory_space=pl.ANY)],
        out_specs=pl.BlockSpec(memory_space=pltpu.VMEM),
        scratch_shapes=[
            vmem((CELLS, GENES), f32),
            vmem((N_CELL, 16, 128), f32),
            vmem((N_X, CELLS, GENES), bf16),
            vmem((2, GENES // 2, CELLS), f32),
            vmem((N_X, 2, PART // 2, CELLS), bf16),
            vmem((8, 128), f32),
            vmem((SLOTS, 8, 128), f32),
            vmem((SLOTS, N_X, 2, PART // 2, CELLS), bf16),
            vmem((4 * CELLS * N_X, GENES), bf16),
            vmem(((SLOTS + 1) * PART, 4 * CELLS * N_X), bf16),
            vmem((SLOTS, 2, 2, ROWS, GENES), f32),
            vmem((SLOTS, 2, ROWS, GENES), f32),
            vmem((SLOTS, 2, ROWS, GENES), f32),
            vmem((SLOTS, 2, ROWS, GENES), f32),
            vmem((SLOTS + 1, N_CHIP, 2, ROWS, PART), f32),
            vmem((SLOTS + 1, N_CHIP, ROWS, PART), f32),
            vmem((SLOTS + 1, N_CHIP, ROWS, PART), f32),
            vmem((SLOTS + 1, N_CHIP, ROWS, PART), f32),
            vmem((SLOTS * PART, GENES), f32),
            vmem((GENES, GENES), f32),
            dma,
            dma((2,)),
            dma((2,)),
            dma((4,)),
            dma((SLOTS,)),
            dma((SLOTS, N_X)),
            dma((SLOTS,)),
            dma((SLOTS,)),
            dma((SLOTS + 1,)),
            dma((SLOTS + 1,)),
            dma((SLOTS + 1,)),
            dma((SLOTS + 1,)),
            dma((SLOTS,)),
            dma((SLOTS,)),
            dma((SLOTS,)),
            dma((SLOTS,)),
        ],
        compiler_params=pltpu.CompilerParams(
            collective_id=0, has_side_effects=True, vmem_limit_bytes=54784 * 1024
        ),
        name="banded_correlation",
    )(expression)


def solution(mesh):
    return jax.shard_map(
        on_device,
        mesh=mesh,
        in_specs=(P("cell", "gene"),),
        out_specs=P(("gene", "cell"), None),
        check_vma=False,
    )
```

```python
import jax
import jax.numpy as jnp
from jax import lax
from jax.experimental import pallas as pl
from jax.experimental.pallas import tpu as pltpu
from jax.sharding import PartitionSpec as P

EPS = 1e-05
MESH = pl.DeviceIdType.MESH
N_GENE, N_CELL, N_CHIP, N_X, N_Y = 32, 16, 8, 4, 8
GENES, CELLS, ROWS, PART = 384, 256, 24, 96
TOTAL = float(CELLS * N_CELL)
SLOTS = 3
SLOT_ORDER = (0, 2, 1)
NEAR = (3, -3, 2, -2, 1, -1)
FAR_FIRST = (12, 13, 11, 4, 5, 3, 10, 9, 14, 6, 7, 2, 8, 15, 1)


def power_of_two(power):
    size = jnp.abs(power).astype(jnp.int32)
    up = jnp.ones_like(power)
    down = jnp.ones_like(power)
    for bit in range(7):
        on = (size & (1 << bit)) != 0
        up = jnp.where(on, up * 2.0 ** (1 << bit), up)
        down = jnp.where(on, down * 2.0 ** -(1 << bit), down)
    return jnp.where(power < 0, down, up)


def lanes(rows):
    return jnp.concatenate([rows[i : i + 1] for i in range(3)], axis=1)


def kernel(
    x_hbm, out_ref, x_ref, gathered, block, flat, quarter, powers, far_powers, partner, left,
    right, turned, turned_sibling, turned_pair, crossed, prod, sibling, paired, arrived,
    begun, row_scale,
    x_sem, stat_sems, own_send, own_recv, gene_send, gene_recv, power_send, power_recv,
    core_send, core_recv, sum_send, sum_recv, flip_send, flip_recv, turn_send, turn_recv,
):
    gene = lax.axis_index("gene")
    cell = lax.axis_index("cell")
    core = lax.rem(cell, 2)
    chip = lax.div(cell, 2)
    x_at = lax.rem(chip, N_X)
    z_at = lax.div(chip, N_X)
    even = lax.rem(gene, 2) == 0
    place_y = lax.rem(gene, N_Y)

    def by_place(for_even, for_odd, **special):
        value = jnp.where(even, for_even, for_odd)
        for name, other in special.items():
            value = jnp.where(place_y == int(name[1:]), other, value)
        return value

    here = [by_place(1, 3, y7=2), by_place(-1, -3, y2=-3), by_place(2, -2, y1=1)]
    back = [by_place(0, 0, y7=1), by_place(1, 1, y2=2), by_place(2, 2, y1=0)]
    away = [by_place(-3, -1, y2=-1), by_place(3, 1, y1=-2), by_place(-2, 2, y7=3)]
    slot_there = [by_place(0, 0, y2=2), by_place(1, 1, y1=0), by_place(2, 2, y7=1)]

    def at(offset):
        return lax.rem(gene + offset + N_GENE, N_GENE)

    def rank(z, x, core):
        return z * (2 * N_X) + x * 2 + core

    def remote(src, dst, send, recv, gene_to, cell_to):
        return pltpu.make_async_remote_copy(
            src_ref=src,
            dst_ref=dst,
            send_sem=send,
            recv_sem=recv,
            device_id=(gene_to, cell_to),
            device_id_type=MESH,
        )

    def wait_bytes(ref, sem):
        pltpu.make_async_copy(ref, ref, sem).wait()

    load = pltpu.make_async_copy(x_hbm, x_ref, x_sem)
    load.start()
    barrier = pltpu.get_barrier_semaphore()

    def greet(gene_to, cell_to):
        pl.semaphore_signal(barrier, inc=1, device_id=(gene_to, cell_to), device_id_type=MESH)

    for offset in NEAR:
        for z in range(2):
            greet(at(offset), rank(z, x_at, core))
    for step in range(1, N_CELL):
        greet(gene, lax.rem(cell + step, N_CELL))

    load.wait()
    x = x_ref[...]
    mean = jnp.sum(x, axis=0, keepdims=True) * (1.0 / CELLS)
    centred = x - mean
    rows = [
        mean,
        jnp.sum(centred * centred, axis=0, keepdims=True),
        jnp.max(x, axis=0, keepdims=True),
        jnp.min(x, axis=0, keepdims=True),
    ]
    parts = [row[:, 128 * i : 128 * i + 128] for row in rows for i in range(3)]
    gathered[cell] = jnp.concatenate(parts + [jnp.zeros((4, 128), jnp.float32)], axis=0)

    pl.semaphore_wait(barrier, N_CELL - 1 + len(NEAR) * 2)

    for step in FAR_FIRST:
        remote(
            gathered.at[cell], gathered.at[cell], stat_sems.at[0], stat_sems.at[1],
            gene, lax.rem(cell + step, N_CELL),
        ).start()
    many = gathered.at[pl.ds(0, N_CELL - 1)]
    wait_bytes(many, stat_sems.at[1])

    total = gathered[0][0:3]
    for i in range(1, N_CELL):
        total = total + gathered[i][0:3]
    mean3 = total * (1.0 / N_CELL)
    inner = jnp.zeros_like(mean3)
    outer = jnp.zeros_like(mean3)
    high = gathered[0][6:9]
    low = gathered[0][9:12]
    for i in range(N_CELL):
        inner = inner + gathered[i][3:6]
        shift = gathered[i][0:3] - mean3
        outer = outer + shift * shift
        high = jnp.maximum(high, gathered[i][6:9])
        low = jnp.minimum(low, gathered[i][9:12])
    spread = inner + outer * float(CELLS)
    deviation = jnp.sqrt(spread * (1.0 / TOTAL) + EPS)
    peak = jnp.maximum(jnp.abs((high - mean3) / deviation), jnp.abs((low - mean3) / deviation))
    power3 = jnp.ceil(jnp.log2(peak))
    scale3 = power_of_two(-power3)
    gain3 = power_of_two(power3)
    gain = lanes(gain3)

    standard = (x_ref[...] - lanes(mean3)) / lanes(deviation)
    value = jnp.floor((standard * lanes(scale3)) * 256.0)
    block[x_at] = value.astype(jnp.bfloat16)
    powers[...] = jnp.concatenate([gain3, jnp.zeros((5, 128), jnp.float32)], axis=0)

    x_of = [lax.rem(x_at + step, N_X) for step in range(N_X)]
    mine = block.at[x_at]
    for step, side in ((1, 0), (3, 1)):
        remote(
            mine, mine, own_send.at[0], own_recv.at[side], gene, rank(z_at, x_of[step], core)
        ).start()
    part_rows = pl.ds(pl.multiple_of(x_at * (PART // 2), 8), PART // 2)

    def send_quarter(step, values):
        flat[...] = values.T.reshape(2, GENES // 2, CELLS)
        quarter[step] = flat[:, part_rows].astype(jnp.bfloat16)
        for slot in range(SLOTS):
            remote(
                quarter.at[step], partner.at[slot_there[slot], step], gene_send.at[slot],
                gene_recv.at[slot_there[slot], step], at(away[slot]), cell,
            ).start()

    send_quarter(0, value)
    for slot in range(SLOTS):
        remote(
            powers, far_powers.at[slot_there[slot]], power_send.at[slot],
            power_recv.at[slot_there[slot]], at(away[slot]), cell,
        ).start()

    wide = jnp.broadcast_to(gain * (2.0**-10 / TOTAL), (128, GENES)).T
    row_scale[...] = jnp.concatenate([wide, wide, wide], axis=1)
    mine_rows = pl.ds(pl.multiple_of(cell * ROWS, 8), ROWS)

    def levels(value):
        fourth = value.astype(jnp.float32)
        third = jnp.floor(fourth * 0.25)
        second = jnp.floor(third * 0.25)
        return fourth, third, second, jnp.floor(second * 0.25)

    chunk = 4 * CELLS
    order = (0, 3, 1, 2)

    def spread_out(step, values):
        fourth, third, second, first = levels(values)
        slices = (first, second - 4.0 * first, third - 4.0 * second, fourth - 4.0 * third)
        for i, piece in enumerate(slices):
            start = chunk * order.index(step) + CELLS * i
            left[start : start + CELLS, :] = piece.astype(jnp.bfloat16)

    def sums_of(ref, row, piece, step):
        for i, level in enumerate(levels(piece.reshape(PART, CELLS))):
            start = chunk * order.index(step) + CELLS * i
            ref[row : row + PART, start : start + CELLS] = level.astype(jnp.bfloat16)

    spread_out(0, value)
    half = CELLS // 2
    for side, came, to in ((0, 3, 1), (1, 1, 3)):
        wait_bytes(block.at[0], own_recv.at[side])
        piece = block.at[x_of[came], pl.ds(side * half, half)]
        remote(
            piece, piece, own_send.at[1], own_recv.at[2 + side], gene, rank(z_at, x_of[to], core)
        ).start()
        send_quarter(came, block[x_of[came]].astype(jnp.float32))
    for step in (3, 1):
        spread_out(step, block[x_of[step]])
    for side in range(2):
        wait_bytes(block.at[0, pl.ds(0, half)], own_recv.at[2 + side])
    send_quarter(2, block[x_of[2]].astype(jnp.float32))
    spread_out(2, block[x_of[2]])

    twin = rank(z_at, x_at, 1 - core)

    copies = {}

    early = chunk * (N_X - 1)

    def product(rows, columns):
        return jnp.dot(right[rows, columns], left[columns], preferred_element_type=jnp.float32)

    def multiply(unit):
        rows = slice(PART * unit, PART * (unit + 1))
        if unit == SLOTS:
            c = product(rows, slice(None))
        else:
            c = begun[rows] + product(rows, slice(early, None))
        if unit < SLOTS:
            turned[unit] = (c * gain).reshape(2, 2, ROWS, GENES)
            copies["flip", unit] = remote(
                turned.at[unit, :, 1 - core], turned_sibling.at[unit],
                flip_send.at[unit], flip_recv.at[unit], gene, twin,
            )
            copies["flip", unit].start()
        prod[unit] = c.T.reshape(N_CHIP, 2, ROWS, PART)
        copies["core", unit] = remote(
            prod.at[unit, :, 1 - core], sibling.at[unit],
            core_send.at[unit], core_recv.at[unit], gene, twin,
        )
        copies["core", unit].start()

    def pair_up(unit):
        if unit < SLOTS:
            copies["flip", unit].wait_recv()
            turned_pair[unit] = turned[unit, :, core] + turned_sibling[unit]
            for z in range(2):
                remote(
                    turned_pair.at[unit, z], crossed.at[back[unit], z_at], turn_send.at[unit],
                    turn_recv.at[back[unit]], at(here[unit]), rank(z, x_at, core),
                ).start()
        copies["core", unit].wait_recv()
        paired[unit] = prod[unit, :, core] + sibling[unit]
        arrived[unit, chip] = paired[unit, chip]
        for step in range(1, N_CHIP):
            there = lax.rem(chip + step, N_CHIP)
            remote(
                paired.at[unit, there], arrived.at[unit, chip],
                sum_send.at[unit], sum_recv.at[unit], gene, there * 2 + core,
            ).start()

    for step in order:
        sums_of(right, PART * SLOTS, quarter[step], step)
    multiply(SLOTS)

    def take(slot, step):
        wait_bytes(partner.at[slot, step], gene_recv.at[slot, step])
        sums_of(right, PART * slot, partner[slot, step], step)

    for step in order[:-1]:
        for slot in SLOT_ORDER:
            take(slot, step)
    begun[...] = product(slice(0, PART * SLOTS), slice(0, early))
    for i, slot in enumerate(SLOT_ORDER):
        take(slot, order[-1])
        multiply(slot)
        pair_up(SLOT_ORDER[i - 1] if i else SLOTS)
    pair_up(SLOT_ORDER[-1])

    def place(offset, value):
        start = pl.multiple_of((offset + 3) * GENES, 128)
        out_ref[:, pl.ds(start, GENES)] = value

    others = pl.ds(0, N_CHIP - 1)

    def keep(unit, offset, far_gain):
        wait_bytes(arrived.at[unit, others], sum_recv.at[unit])
        quarters = [arrived[unit, x] + arrived[unit, N_X + x] for x in range(N_X)]
        size = PART // 2
        total = jnp.concatenate(
            [q[:, size * z : size * (z + 1)] for z in range(2) for q in quarters], axis=1
        )
        place(offset, total * (row_scale[mine_rows, :] * far_gain))

    keep(SLOTS, 0, gain)
    for slot in SLOT_ORDER:
        wait_bytes(far_powers.at[slot], power_recv.at[slot])
        keep(slot, here[slot], lanes(far_powers[slot][0:3]))
    for slot in range(SLOTS):
        wait_bytes(crossed.at[slot], turn_recv.at[slot])
        place(away[slot], (crossed[slot, 0] + crossed[slot, 1]) * row_scale[mine_rows, :])

    wait_bytes(many, stat_sems.at[0])
    wait_bytes(block.at[pl.ds(0, 2)], own_send.at[0])
    wait_bytes(block.at[0], own_send.at[1])
    for unit in range(SLOTS + 1):
        if unit < SLOTS:
            wait_bytes(quarter, gene_send.at[unit])
            wait_bytes(powers, power_send.at[unit])
            wait_bytes(turned_pair.at[unit], turn_send.at[unit])
            copies["flip", unit].wait_send()
        copies["core", unit].wait_send()
        wait_bytes(arrived.at[unit, others], sum_send.at[unit])


def on_device(expression):
    f32, bf16 = jnp.float32, jnp.bfloat16
    vmem, dma = pltpu.VMEM, pltpu.SemaphoreType.DMA
    return pl.pallas_call(
        kernel,
        out_shape=jax.ShapeDtypeStruct((ROWS, 7 * GENES), f32),
        in_specs=[pl.BlockSpec(memory_space=pl.ANY)],
        out_specs=pl.BlockSpec(memory_space=pltpu.VMEM),
        scratch_shapes=[
            vmem((CELLS, GENES), f32),
            vmem((N_CELL, 16, 128), f32),
            vmem((N_X, CELLS, GENES), bf16),
            vmem((2, GENES // 2, CELLS), f32),
            vmem((N_X, 2, PART // 2, CELLS), bf16),
            vmem((8, 128), f32),
            vmem((SLOTS, 8, 128), f32),
            vmem((SLOTS, N_X, 2, PART // 2, CELLS), bf16),
            vmem((4 * CELLS * N_X, GENES), bf16),
            vmem(((SLOTS + 1) * PART, 4 * CELLS * N_X), bf16),
            vmem((SLOTS, 2, 2, ROWS, GENES), f32),
            vmem((SLOTS, 2, ROWS, GENES), f32),
            vmem((SLOTS, 2, ROWS, GENES), f32),
            vmem((SLOTS, 2, ROWS, GENES), f32),
            vmem((SLOTS + 1, N_CHIP, 2, ROWS, PART), f32),
            vmem((SLOTS + 1, N_CHIP, ROWS, PART), f32),
            vmem((SLOTS + 1, N_CHIP, ROWS, PART), f32),
            vmem((SLOTS + 1, N_CHIP, ROWS, PART), f32),
            vmem((SLOTS * PART, GENES), f32),
            vmem((GENES, GENES), f32),
            dma,
            dma((2,)),
            dma((2,)),
            dma((4,)),
            dma((SLOTS,)),
            dma((SLOTS, N_X)),
            dma((SLOTS,)),
            dma((SLOTS,)),
            dma((SLOTS + 1,)),
            dma((SLOTS + 1,)),
            dma((SLOTS + 1,)),
            dma((SLOTS + 1,)),
            dma((SLOTS,)),
            dma((SLOTS,)),
            dma((SLOTS,)),
            dma((SLOTS,)),
        ],
        compiler_params=pltpu.CompilerParams(
            collective_id=0, has_side_effects=True, vmem_limit_bytes=54784 * 1024
        ),
        name="banded_correlation",
    )(expression)


def solution(mesh):
    return jax.shard_map(
        on_device,
        mesh=mesh,
        in_specs=(P("cell", "gene"),),
        out_specs=P(("gene", "cell"), None),
        check_vma=False,
    )
```
